32 devices in a mesh: tm: 8 (over y, x, core), space: 4 (over z).
Axes of the slice: x: 2, y: 2, z: 4, core: 2. Of those that a mesh axis runs over, the one named last changes fastest.
Arguments:
- video: bfloat16 [32, 1152, 1536], P('tm', 'space'), may hold values from -6 to 6
- frame_count: int32 [1], replicated, may hold values from 8 to 32
- qkv_space: bfloat16 [1536, 3072], replicated, may hold values from -0.15625 to 0.15625
- out_space: bfloat16 [1024, 1536], replicated, may hold values from -0.1875 to 0.1875
- qkv_time: bfloat16 [1536, 3072], replicated, may hold values from -0.15625 to 0.15625
- out_time: bfloat16 [1024, 1536], replicated, may hold values from -0.1875 to 0.1875
Outputs:
- encoded: bfloat16 [32, 1152, 1536], P('tm', 'space')
The draws below stay inside these ranges and needn't reach their ends.
All inputs are finite; a program needn't handle non-finite values.
Results may differ from the reference program's by a relative error of at most 0.0085.
Values may be sent and summed in bfloat16 or wider, within the bound.
A program may use at most 192 MiB of HBM per device.

```python
import jax
import jax.numpy as jnp
from jax import lax

D = 1536
H = 16
HD = 64
PATCHES = 1152
FRAMES = 32


def block_scale(own_key, extent, pieces, low, top_value):
    level = 1.0
    for position, shards_of in pieces:
        steps = jax.random.uniform(jax.random.fold_in(jax.random.fold_in(own_key, 6), position), (shards_of,), jnp.float32, low / len(pieces), top_value / len(pieces))
        level = level * jnp.repeat(jnp.exp(steps), extent[position] // shards_of).reshape((-1,) + (1,) * (len(extent) - 1 - position))
    return level


def centred(key, shape, deviation, reach, cuts=(), held_as=jnp.bfloat16):
    drawn = jax.random.normal(key, shape, jnp.float32) * deviation
    if len(cuts) > 0:
        drawn = block_scale(key, shape, cuts, -0.22, 0.18) * drawn
    return jnp.clip(drawn, min=-reach, max=reach).astype(held_as)


def setup_inputs(seed: int = 0) -> dict:
    splits = jax.random.split(jax.random.key(seed), 7)
    video = centred(splits[0], (FRAMES, PATCHES, D), 1.0, 6.0, ((0, 8), (1, 4)))
    frame_count = jax.random.randint(splits[1], (1,), FRAMES // 4, FRAMES + 1).astype(jnp.int32)
    qkv_space = centred(splits[2], (D, 3 * H * HD), D ** -0.5, 0.15625)
    out_space = centred(splits[3], (H * HD, D), (H * HD) ** -0.5, 0.1875)
    qkv_time = centred(splits[4], (D, 3 * H * HD), D ** -0.5, 0.15625)
    out_time = centred(splits[5], (H * HD, D), (H * HD) ** -0.5, 0.1875)
    return dict(video=video, frame_count=frame_count, qkv_space=qkv_space, out_space=out_space, qkv_time=qkv_time, out_time=out_time)


def layer_norm(values):
    wide = values.astype(jnp.float32)
    center = wide - lax.optimization_barrier(jnp.mean(wide, axis=-1, keepdims=True))
    spread = lax.optimization_barrier(jnp.mean(center * center, axis=-1, keepdims=True))
    return (center * lax.rsqrt(spread + 1e-06)).astype(jnp.bfloat16)

def reference(video, frame_count, qkv_space, out_space, qkv_time, out_time):
    frames, patches, width = video.shape
    valid_keys = jnp.arange(frames) < frame_count[0]
    valid = valid_keys.astype(jnp.float32)[:, None, None]
    norm1 = layer_norm(video)
    qkv1 = jnp.dot(norm1.reshape(frames * patches, width), qkv_space, preferred_element_type=jnp.float32)
    qkv1 = qkv1.astype(jnp.bfloat16).reshape(frames, patches, 3, H, HD)

    def frame_attend(item):
        query = item[:, 0].astype(jnp.float32)
        keys = item[:, 1].astype(jnp.float32)
        values = item[:, 2].astype(jnp.float32)
        scores = jnp.einsum('qhd,khd->hqk', query, keys) * 0.125
        weights = jax.nn.softmax(scores, axis=-1).astype(jnp.bfloat16)
        result = jnp.einsum('hqk,khd->qhd', weights.astype(jnp.float32), values)
        return result.astype(jnp.bfloat16).reshape(patches, H * HD)
    spatial = lax.map(frame_attend, qkv1)
    branch = jnp.dot(spatial.reshape(frames * patches, H * HD), out_space, preferred_element_type=jnp.float32)
    middle = (video.astype(jnp.float32) + valid * branch.reshape(frames, patches, width)).astype(jnp.bfloat16)
    norm2 = layer_norm(middle)
    qkv2 = jnp.dot(norm2.reshape(frames * patches, width), qkv_time, preferred_element_type=jnp.float32)
    qkv2 = qkv2.astype(jnp.bfloat16).reshape(frames, patches, 3, H, HD)
    query = qkv2[:, :, 0].astype(jnp.float32)
    keys = qkv2[:, :, 1].astype(jnp.float32)
    values = qkv2[:, :, 2].astype(jnp.float32)
    scores = jnp.einsum('fphd,gphd->phfg', query, keys) * 0.125
    scores = jnp.where(valid_keys[None, None, None, :], scores, -1e+30)
    weights = jax.nn.softmax(scores, axis=-1).astype(jnp.bfloat16)
    temporal = jnp.einsum('phfg,gphd->fphd', weights.astype(jnp.float32), values)
    temporal = temporal.astype(jnp.bfloat16).reshape(frames * patches, H * HD)
    branch2 = jnp.dot(temporal, out_time, preferred_element_type=jnp.float32).reshape(frames, patches, width)
    return (middle.astype(jnp.float32) + valid * branch2).astype(jnp.bfloat16)
```

```python
import functools
import math

import jax
import jax.numpy as jnp
from jax import lax
from jax.experimental import pallas as pl
from jax.experimental.pallas import tpu as pltpu
from jax.sharding import PartitionSpec as P

H = 16
HD = 64
BF = jnp.bfloat16
F32 = jnp.float32
VMEM_LIMIT = 56 * 1024 * 1024
LOG2E = 1.0 / math.log(2.0)


def layer_norm(values):
    wide = values.astype(jnp.float32)
    center = wide - jnp.mean(wide, axis=-1, keepdims=True)
    spread = jnp.mean(center * center, axis=-1, keepdims=True)
    return (center * lax.rsqrt(spread + 1e-06)).astype(jnp.bfloat16)


def spatial_attend(items):
    count = items.shape[0]
    total = items.shape[1]
    local_heads = items.shape[3] // HD
    parts = items.reshape(count, total, 3, local_heads, HD)
    scores = (
        jnp.einsum(
            "fqhd,fkhd->fhqk", parts[:, :, 0], parts[:, :, 1], preferred_element_type=jnp.float32
        )
        * 0.125
    )
    weights = jax.nn.softmax(scores, axis=-1).astype(jnp.bfloat16)
    result = jnp.einsum(
        "fhqk,fkhd->fqhd", weights, parts[:, :, 2], preferred_element_type=jnp.float32
    )
    result = result.astype(jnp.bfloat16).reshape(count, total, local_heads * HD)
    return lax.all_to_all(result, "space", split_axis=1, concat_axis=2, tiled=True)


def general(video, frame_count, qkv_space, out_space, qkv_time, out_time):
    frames, patches, width = video.shape
    first = lax.axis_index("tm") * frames
    limit = frame_count[0]
    valid = (first + jnp.arange(frames) < limit).astype(jnp.float32)[:, None, None]
    norm1 = layer_norm(video)
    qkv1 = jnp.dot(
        norm1.reshape(frames * patches, width), qkv_space, preferred_element_type=jnp.float32
    )
    qkv1 = qkv1.astype(jnp.bfloat16).reshape(frames, patches, 3, H * HD)
    spatial = spatial_attend(lax.all_to_all(qkv1, "space", split_axis=3, concat_axis=1, tiled=True))
    branch = jnp.dot(
        spatial.reshape(frames * patches, H * HD), out_space, preferred_element_type=jnp.float32
    )
    middle = (video.astype(jnp.float32) + valid * branch.reshape(frames, patches, width)).astype(
        jnp.bfloat16
    )
    norm2 = layer_norm(middle)
    qkv2 = jnp.dot(
        norm2.reshape(frames * patches, width), qkv_time, preferred_element_type=jnp.float32
    )
    qkv2 = qkv2.astype(jnp.bfloat16).reshape(frames, patches, 3 * H * HD)
    gathered = lax.all_to_all(qkv2, "tm", split_axis=1, concat_axis=0, tiled=True)
    all_frames, few_patches = (gathered.shape[0], gathered.shape[1])
    parts = gathered.reshape(all_frames, few_patches, 3, H, HD)
    scores = (
        jnp.einsum(
            "fphd,gphd->phfg", parts[:, :, 0], parts[:, :, 1], preferred_element_type=jnp.float32
        )
        * 0.125
    )
    key_valid = jnp.arange(all_frames) < limit
    scores = jnp.where(key_valid[None, None, None, :], scores, -1e30)
    weights = jax.nn.softmax(scores, axis=-1).astype(jnp.bfloat16)
    temporal = jnp.einsum(
        "phfg,gphd->fphd", weights, parts[:, :, 2], preferred_element_type=jnp.float32
    )
    temporal = temporal.astype(jnp.bfloat16).reshape(all_frames, few_patches, H * HD)
    returned = lax.all_to_all(temporal, "tm", split_axis=0, concat_axis=1, tiled=True)
    branch2 = jnp.dot(
        returned.reshape(frames * patches, H * HD), out_time, preferred_element_type=jnp.float32
    )
    return (middle.astype(jnp.float32) + valid * branch2.reshape(frames, patches, width)).astype(
        jnp.bfloat16
    )


def pair_softmax(query, key, value, low, mask, rows):
    query = (query.astype(F32) * (0.125 * LOG2E)).astype(BF)
    zero, one = jnp.zeros_like(query), jnp.ones_like(value)
    queries = (jnp.where(low, query, zero), jnp.where(low, zero, query))
    values = (jnp.where(low, value, one), jnp.where(low, one, value))
    total = query.shape[0]
    out = []
    for start in range(0, total, rows):
        sums = []
        for head in range(2):
            scores = lax.dot_general(
                queries[head][start : start + rows],
                key,
                (((1,), (1,)), ((), ())),
                preferred_element_type=F32,
            )
            if mask is not None:
                scores = jnp.where(mask, scores, -1e30)
            top = jnp.max(scores, axis=1, keepdims=True)
            weights = jnp.exp2((scores - top).astype(BF))
            sums.append(jnp.dot(weights, values[head], preferred_element_type=F32))
        half = low[start : start + rows]
        result = jnp.where(half, sums[0], sums[1])
        norm = pltpu.roll(jnp.where(half, sums[1], sums[0]), HD, 1)
        out.append((result / norm).astype(BF))
    return out


def norm_rows(wide):
    center = wide - jnp.mean(wide, axis=-1, keepdims=True)
    spread = jnp.mean(center * center, axis=-1, keepdims=True)
    return (center * lax.rsqrt(spread + 1e-06)).astype(BF)


def space_kernel(rows, x_ref, wq_ref, wk_ref, wv_ref, out_ref, norm_ref):
    total = x_ref.shape[0]

    @pl.when(pl.program_id(0) == 0)
    def _():
        @pl.loop(0, total // 96)
        def _(i):
            part = pl.ds(pl.multiple_of(i * 96, 96), 96)
            norm_ref[part, :] = norm_rows(x_ref[part, :].astype(F32))

    normed = norm_ref[...]
    query = jnp.dot(normed, wq_ref[...], preferred_element_type=F32).astype(BF)
    key = jnp.dot(normed, wk_ref[...], preferred_element_type=F32).astype(BF)
    value = jnp.dot(normed, wv_ref[...], preferred_element_type=F32).astype(BF)
    low = lax.broadcasted_iota(jnp.int32, (total, 2 * HD), 1) < HD
    for pair in range(query.shape[1] // (2 * HD)):
        cols = slice(pair * 2 * HD, (pair + 1) * 2 * HD)
        out = pair_softmax(query[:, cols], key[:, cols], value[:, cols], low, None, rows)
        for i, block in enumerate(out):
            out_ref[i * rows : (i + 1) * rows, cols] = block


def space_attention(frame, weights):
    total, width = frame.shape
    groups = 4
    cols = H * HD // groups
    return pl.pallas_call(
        functools.partial(space_kernel, 288),
        grid=(groups,),
        in_specs=[
            pl.BlockSpec((total, width), lambda i: (0, 0)),
            pl.BlockSpec((width, cols), lambda i: (0, i)),
            pl.BlockSpec((width, cols), lambda i: (0, groups + i)),
            pl.BlockSpec((width, cols), lambda i: (0, 2 * groups + i)),
        ],
        out_specs=pl.BlockSpec((total, cols), lambda i: (0, i)),
        out_shape=jax.ShapeDtypeStruct((total, H * HD), BF),
        scratch_shapes=[pltpu.VMEM((total, width), BF)],
        compiler_params=pltpu.CompilerParams(vmem_limit_bytes=VMEM_LIMIT),
        cost_estimate=pl.CostEstimate(
            flops=2 * total * width * 3 * H * HD + 4 * total * total * H * HD,
            bytes_accessed=2 * (total * width + 3 * width * H * HD + total * H * HD),
            transcendentals=total * total * H,
        ),
    )(frame, weights, weights, weights)


def interleave(values):
    frames, patches, width = values.shape
    parts = values.reshape(frames, patches // 8, 8, width)
    pieces = []
    for half in range(2):
        for f in range(frames):
            pieces.append(parts[f][:, half * 4 : half * 4 + 4])
    return jnp.concatenate(pieces, axis=1).reshape(frames * patches, width)


def deinterleave(values, frames):
    rows, width = values.shape
    parts = values.reshape(rows // (8 * frames), 8 * frames, width)
    out = []
    for f in range(frames):
        first = parts[:, f * 4 : f * 4 + 4]
        second = parts[:, 4 * frames + f * 4 : 4 * frames + f * 4 + 4]
        out.append(jnp.concatenate([first, second], axis=1).reshape(rows // frames, width))
    return out


def middle_kernel(count_ref, x_ref, s_ref, w_ref, out_ref):
    frames, patches, width = x_ref.shape
    branch = jnp.dot(
        s_ref[...].reshape(frames * patches, s_ref.shape[2]), w_ref[...], preferred_element_type=F32
    ).reshape(frames, patches, width)
    first = lax.axis_index("tm") * frames
    parts = []
    for f in range(frames):
        valid = (first + f < count_ref[0]).astype(F32)
        parts.append(x_ref[f].astype(F32) + valid * branch[f])
    out_ref[...] = interleave(jnp.stack(parts)).astype(BF)


def middle_rows(frame_count, video, spatial, weights):
    frames, patches, width = video.shape
    step = 96
    return pl.pallas_call(
        middle_kernel,
        grid=(patches // step,),
        in_specs=[
            pl.BlockSpec(memory_space=pltpu.SMEM),
            pl.BlockSpec((frames, step, width), lambda i: (0, i, 0)),
            pl.BlockSpec((frames, step, H * HD), lambda i: (0, i, 0)),
            pl.BlockSpec((H * HD, width), lambda i: (0, 0)),
        ],
        out_specs=pl.BlockSpec((frames * step, width), lambda i: (i, 0)),
        out_shape=jax.ShapeDtypeStruct((frames * patches, width), BF),
        compiler_params=pltpu.CompilerParams(vmem_limit_bytes=VMEM_LIMIT),
    )(frame_count, video, spatial, weights)


def time_kernel(count_ref, x_ref, w_ref, out_ref):
    sources, groups, rows, width = x_ref.shape
    total = sources * rows
    normed = jnp.concatenate(
        [norm_rows(x_ref[:, g].reshape(total, width).astype(F32)) for g in range(groups)], axis=0
    )
    qkv = jnp.dot(normed, w_ref[...], preferred_element_type=F32).astype(BF)
    low = lax.broadcasted_iota(jnp.int32, (total, 2 * HD), 1) < HD
    row = lax.broadcasted_iota(jnp.int32, (total, total), 0)
    col = lax.broadcasted_iota(jnp.int32, (total, total), 1)
    mask = (row % 4 == col % 4) & (col // 4 < count_ref[0])
    for g in range(groups):
        own = qkv[g * total : (g + 1) * total]
        for pair in range(H // 2):
            parts = [
                own[:, k * H * HD + pair * 2 * HD : k * H * HD + (pair + 1) * 2 * HD]
                for k in range(3)
            ]
            (result,) = pair_softmax(*parts, low, mask, total)
            out_ref[:, g, :, pair * 2 * HD : (pair + 1) * 2 * HD] = result.reshape(
                sources, rows, 2 * HD
            )


def time_attention(frame_count, middle, weights):
    sources, groups, rows, width = middle.shape
    step = 3
    return pl.pallas_call(
        time_kernel,
        grid=(groups // step,),
        in_specs=[
            pl.BlockSpec(memory_space=pltpu.SMEM),
            pl.BlockSpec((sources, step, rows, width), lambda i: (0, i, 0, 0)),
            pl.BlockSpec((width, 3 * H * HD), lambda i: (0, 0)),
        ],
        out_specs=pl.BlockSpec((sources, step, rows, H * HD), lambda i: (0, i, 0, 0)),
        out_shape=jax.ShapeDtypeStruct((sources, groups, rows, H * HD), BF),
        compiler_params=pltpu.CompilerParams(vmem_limit_bytes=VMEM_LIMIT),
    )(frame_count, middle, weights)


def final_kernel(count_ref, m_ref, t_ref, w_ref, out_ref):
    frames, patches, width = out_ref.shape
    branch = jnp.dot(t_ref[...], w_ref[...], preferred_element_type=F32)
    first = lax.axis_index("tm") * frames
    middles = deinterleave(m_ref[...].astype(F32), frames)
    branches = deinterleave(branch, frames)
    for f in range(frames):
        valid = (first + f < count_ref[0]).astype(F32)
        out_ref[f] = (middles[f] + valid * branches[f]).astype(BF)


def final_rows(frame_count, middle, temporal, weights, frames):
    rows, width = middle.shape
    patches = rows // frames
    step = 96
    return pl.pallas_call(
        final_kernel,
        grid=(patches // step,),
        in_specs=[
            pl.BlockSpec(memory_space=pltpu.SMEM),
            pl.BlockSpec((frames * step, width), lambda i: (i, 0)),
            pl.BlockSpec((frames * step, H * HD), lambda i: (i, 0)),
            pl.BlockSpec((H * HD, width), lambda i: (0, 0)),
        ],
        out_specs=pl.BlockSpec((frames, step, width), lambda i: (0, i, 0)),
        out_shape=jax.ShapeDtypeStruct((frames, patches, width), BF),
        compiler_params=pltpu.CompilerParams(vmem_limit_bytes=VMEM_LIMIT),
    )(frame_count, middle, temporal, weights)


def by_frame(video, frame_count, qkv_space, out_space, qkv_time, out_time):
    frames, patches, width = video.shape
    devices = lax.axis_size("tm")
    frame = lax.all_to_all(video, "space", split_axis=0, concat_axis=0, tiled=True)
    spatial = space_attention(frame.reshape(frames * patches, width), qkv_space)
    spatial = spatial.reshape(frames, patches, H * HD)
    spatial = lax.all_to_all(spatial, "space", split_axis=0, concat_axis=0, tiled=True)
    middle = middle_rows(frame_count, video, spatial, out_space)
    sent = middle.reshape(devices, frames * patches // devices, width)
    sent = lax.all_to_all(sent, "tm", split_axis=0, concat_axis=0, tiled=True)
    temporal = time_attention(frame_count, sent.reshape(devices, -1, 4 * frames, width), qkv_time)
    temporal = temporal.reshape(devices, frames * patches // devices, H * HD)
    temporal = lax.all_to_all(temporal, "tm", split_axis=0, concat_axis=0, tiled=True)
    return final_rows(
        frame_count, middle, temporal.reshape(frames * patches, H * HD), out_time, frames
    )


def per_device(video, *rest):
    frames, patches, _ = video.shape
    fits = (
        frames == 4
        and lax.axis_size("space") == frames
        and lax.axis_size("tm") == 8
        and patches == 288
    )
    return (by_frame if fits else general)(video, *rest)


def solution(mesh):
    return jax.shard_map(
        per_device,
        mesh=mesh,
        in_specs=(P("tm", "space", None), P(), P(), P(), P(), P()),
        out_specs=P("tm", "space", None),
        check_vma=False,
    )
```

```python
import functools
import math

import jax
import jax.numpy as jnp
from jax import lax
from jax.experimental import pallas as pl
from jax.experimental.pallas import tpu as pltpu
from jax.sharding import PartitionSpec as P

H = 16
HD = 64
BF = jnp.bfloat16
F32 = jnp.float32
VMEM_LIMIT = 56 * 1024 * 1024
LOG2E = 1.0 / math.log(2.0)


def layer_norm(values):
    wide = values.astype(jnp.float32)
    center = wide - jnp.mean(wide, axis=-1, keepdims=True)
    spread = jnp.mean(center * center, axis=-1, keepdims=True)
    return (center * lax.rsqrt(spread + 1e-06)).astype(jnp.bfloat16)


def spatial_attend(items):
    count = items.shape[0]
    total = items.shape[1]
    local_heads = items.shape[3] // HD
    parts = items.reshape(count, total, 3, local_heads, HD)
    scores = (
        jnp.einsum(
            "fqhd,fkhd->fhqk", parts[:, :, 0], parts[:, :, 1], preferred_element_type=jnp.float32
        )
        * 0.125
    )
    weights = jax.nn.softmax(scores, axis=-1).astype(jnp.bfloat16)
    result = jnp.einsum(
        "fhqk,fkhd->fqhd", weights, parts[:, :, 2], preferred_element_type=jnp.float32
    )
    result = result.astype(jnp.bfloat16).reshape(count, total, local_heads * HD)
    return lax.all_to_all(result, "space", split_axis=1, concat_axis=2, tiled=True)


def general(video, frame_count, qkv_space, out_space, qkv_time, out_time):
    frames, patches, width = video.shape
    first = lax.axis_index("tm") * frames
    limit = frame_count[0]
    valid = (first + jnp.arange(frames) < limit).astype(jnp.float32)[:, None, None]
    norm1 = layer_norm(video)
    qkv1 = jnp.dot(
        norm1.reshape(frames * patches, width), qkv_space, preferred_element_type=jnp.float32
    )
    qkv1 = qkv1.astype(jnp.bfloat16).reshape(frames, patches, 3, H * HD)
    spatial = spatial_attend(lax.all_to_all(qkv1, "space", split_axis=3, concat_axis=1, tiled=True))
    branch = jnp.dot(
        spatial.reshape(frames * patches, H * HD), out_space, preferred_element_type=jnp.float32
    )
    middle = (video.astype(jnp.float32) + valid * branch.reshape(frames, patches, width)).astype(
        jnp.bfloat16
    )
    norm2 = layer_norm(middle)
    qkv2 = jnp.dot(
        norm2.reshape(frames * patches, width), qkv_time, preferred_element_type=jnp.float32
    )
    qkv2 = qkv2.astype(jnp.bfloat16).reshape(frames, patches, 3 * H * HD)
    gathered = lax.all_to_all(qkv2, "tm", split_axis=1, concat_axis=0, tiled=True)
    all_frames, few_patches = (gathered.shape[0], gathered.shape[1])
    parts = gathered.reshape(all_frames, few_patches, 3, H, HD)
    scores = (
        jnp.einsum(
            "fphd,gphd->phfg", parts[:, :, 0], parts[:, :, 1], preferred_element_type=jnp.float32
        )
        * 0.125
    )
    key_valid = jnp.arange(all_frames) < limit
    scores = jnp.where(key_valid[None, None, None, :], scores, -1e30)
    weights = jax.nn.softmax(scores, axis=-1).astype(jnp.bfloat16)
    temporal = jnp.einsum(
        "phfg,gphd->fphd", weights, parts[:, :, 2], preferred_element_type=jnp.float32
    )
    temporal = temporal.astype(jnp.bfloat16).reshape(all_frames, few_patches, H * HD)
    returned = lax.all_to_all(temporal, "tm", split_axis=0, concat_axis=1, tiled=True)
    branch2 = jnp.dot(
        returned.reshape(frames * patches, H * HD), out_time, preferred_element_type=jnp.float32
    )
    return (middle.astype(jnp.float32) + valid * branch2.reshape(frames, patches, width)).astype(
        jnp.bfloat16
    )


def norm_rows(wide):
    center = wide - jnp.mean(wide, axis=-1, keepdims=True)
    spread = jnp.mean(center * center, axis=-1, keepdims=True)
    return (center * lax.rsqrt(spread + 1e-06)).astype(BF)


def space_kernel(video, weights, out, x_buf, w_buf, normed, qkv, sent, sems):
    send_in, recv_in, local, send_out, recv_out, keep = sems
    n, patches, width = x_buf.shape
    chunks, _, _, cols = out.shape
    me = lax.axis_index("space")
    peers = [lax.rem(me + d, n) for d in range(n)]
    froms = [lax.rem(me + n - d, n) for d in range(n)]

    barrier = pltpu.get_barrier_semaphore()
    for d in range(1, n):
        pl.semaphore_signal(
            barrier, inc=1, device_id={"space": peers[d]}, device_id_type=pl.DeviceIdType.MESH
        )
    own = pltpu.make_async_copy(video.at[me], x_buf.at[me], local.at[0])
    own.start()
    load = pltpu.make_async_copy(weights, w_buf, local.at[1])
    load.start()
    pl.semaphore_wait(barrier, n - 1)
    arrivals = []
    for d in range(1, n):
        copy = pltpu.make_async_remote_copy(
            src_ref=video.at[peers[d]],
            dst_ref=x_buf.at[me],
            send_sem=send_in.at[d],
            recv_sem=recv_in.at[d],
            device_id={"space": peers[d]},
            device_id_type=pl.DeviceIdType.MESH,
        )
        copy.start()
        arrivals.append(copy)
    own.wait()
    load.wait()

    def project(source):
        @pl.loop(0, patches // 96)
        def _(i):
            part = pl.ds(pl.multiple_of(i * 96, 96), 96)
            normed[part, :] = norm_rows(x_buf[source, part, :].astype(F32))

        start = pl.multiple_of(source * patches, patches)

        @pl.loop(0, 6)
        def _(i):
            part = pl.ds(pl.multiple_of(i * 512, 512), 512)
            result = jnp.dot(normed[...], w_buf[:, part], preferred_element_type=F32)
            scale = jnp.where(i < 2, 0.125 * LOG2E, 1.0).astype(F32)
            qkv[pl.ds(start, patches), part] = (result * scale).astype(BF)

    project(me)
    for d in range(1, n):
        arrivals[d - 1].wait_recv()
        project(froms[d])

    low = lax.broadcasted_iota(jnp.int32, (patches, 2 * HD), 1) < HD
    low_all = lax.broadcasted_iota(jnp.int32, (n * patches, 2 * HD), 1) < HD

    def outgoing(c, d):
        return pltpu.make_async_remote_copy(
            src_ref=sent.at[c, d],
            dst_ref=out.at[c, me],
            send_sem=send_out.at[c, d],
            recv_sem=recv_out.at[c, d],
            device_id={"space": peers[d]},
            device_id_type=pl.DeviceIdType.MESH,
        )

    @pl.loop(0, chunks)
    def _(c):
        keys, values = [], []
        for pair in range(2):
            start = pl.multiple_of(H * HD + c * cols + pair * 128, 128)
            keys.append(qkv[:, pl.ds(start, 128)])
            start = pl.multiple_of(2 * H * HD + c * cols + pair * 128, 128)
            value = qkv[:, pl.ds(start, 128)]
            one = jnp.ones_like(value)
            values.append((jnp.where(low_all, value, one), jnp.where(low_all, one, value)))
        units = [(d, pair, head) for d in (1, 2, 3, 0) for pair in range(2) for head in range(2)]

        def scores_of(unit):
            d, pair, head = unit
            rows = pl.ds(pl.multiple_of(peers[d] * patches, patches), patches)
            query = qkv[rows, pl.ds(pl.multiple_of(c * cols + pair * 128, 128), 128)]
            zero = jnp.zeros_like(query)
            query = jnp.where(low, query, zero) if head == 0 else jnp.where(low, zero, query)
            return lax.dot_general(
                query, keys[pair], (((1,), (1,)), ((), ())), preferred_element_type=F32
            )

        following = scores_of(units[0])
        sums = []
        for at, (d, pair, head) in enumerate(units):
            scores = following
            if at + 1 < len(units):
                following = scores_of(units[at + 1])
            top = jnp.max(scores, axis=1, keepdims=True)
            exps = jnp.exp2((scores - top).astype(BF))
            sums.append(jnp.dot(exps, values[pair][head], preferred_element_type=F32))
            if head == 1:
                result = jnp.where(low, sums[0], sums[1])
                norm = pltpu.roll(jnp.where(low, sums[1], sums[0]), HD, 1)
                sums = []
                sent[c, d, :, pair * 128 : (pair + 1) * 128] = (result / norm).astype(BF)
                if pair == 1:
                    if d > 0:
                        outgoing(c, d).start()
                    else:
                        pltpu.make_async_copy(sent.at[c, 0], out.at[c, me], keep.at[c]).start()

    for copy in arrivals:
        copy.wait_send()
    for c in range(chunks):
        pltpu.make_async_copy(sent.at[c, 0], out.at[c, me], keep.at[c]).wait()
        for d in range(1, n):
            outgoing(c, d).wait()


def space_attention(video, weights):
    n, patches, width = video.shape
    total = n * patches
    chunks = 4
    cols = H * HD // chunks

    def kernel(v, w, o, x_buf, w_buf, normed, qkv, sent, *sems):
        space_kernel(v, w, o, x_buf, w_buf, normed, qkv, sent, sems)

    return pl.pallas_call(
        kernel,
        in_specs=[pl.BlockSpec(memory_space=pl.ANY)] * 2,
        out_specs=pl.BlockSpec(memory_space=pl.ANY),
        out_shape=jax.ShapeDtypeStruct((chunks, n, patches, cols), BF),
        scratch_shapes=[
            pltpu.VMEM((n, patches, width), BF),
            pltpu.VMEM((width, 3 * H * HD), BF),
            pltpu.VMEM((patches, width), BF),
            pltpu.VMEM((total, 3 * H * HD), BF),
            pltpu.VMEM((chunks, n, patches, cols), BF),
            pltpu.SemaphoreType.DMA((n,)),
            pltpu.SemaphoreType.DMA((n,)),
            pltpu.SemaphoreType.DMA((2,)),
            pltpu.SemaphoreType.DMA((chunks, n)),
            pltpu.SemaphoreType.DMA((chunks, n)),
            pltpu.SemaphoreType.DMA((chunks,)),
        ],
        compiler_params=pltpu.CompilerParams(
            vmem_limit_bytes=VMEM_LIMIT, collective_id=0, has_side_effects=True
        ),
        cost_estimate=pl.CostEstimate(
            flops=2 * total * width * 3 * H * HD + 4 * total * total * H * HD,
            bytes_accessed=2 * (total * width + 3 * width * H * HD + total * H * HD),
            transcendentals=total * total * H,
        ),
    )(video, weights)


def interleave(values):
    frames, patches, width = values.shape
    parts = values.reshape(frames, patches // 8, 8, width)
    pieces = []
    for half in range(2):
        for f in range(frames):
            pieces.append(parts[f][:, half * 4 : half * 4 + 4])
    return jnp.concatenate(pieces, axis=1).reshape(frames * patches, width)


def deinterleave(values, frames):
    rows, width = values.shape
    parts = values.reshape(rows // (8 * frames), 8 * frames, width)
    out = []
    for f in range(frames):
        first = parts[:, f * 4 : f * 4 + 4]
        second = parts[:, 4 * frames + f * 4 : 4 * frames + f * 4 + 4]
        out.append(jnp.concatenate([first, second], axis=1).reshape(rows // frames, width))
    return out


def middle_kernel(count_ref, x_ref, s_ref, w_ref, out_ref):
    frames, patches, width = x_ref.shape
    chunks, _, _, cols = s_ref.shape
    branch = sum(
        jnp.dot(
            s_ref[c].reshape(frames * patches, cols),
            w_ref[c * cols : (c + 1) * cols, :],
            preferred_element_type=F32,
        )
        for c in range(chunks)
    ).reshape(frames, patches, width)
    first = lax.axis_index("tm") * frames
    parts = []
    for f in range(frames):
        valid = (first + f < count_ref[0]).astype(F32)
        parts.append(x_ref[f].astype(F32) + valid * branch[f])
    out_ref[...] = interleave(jnp.stack(parts)).astype(BF)


def middle_rows(frame_count, video, spatial, weights):
    frames, patches, width = video.shape
    step = 96
    return pl.pallas_call(
        middle_kernel,
        grid=(patches // step,),
        in_specs=[
            pl.BlockSpec(memory_space=pltpu.SMEM),
            pl.BlockSpec((frames, step, width), lambda i: (0, i, 0)),
            pl.BlockSpec((spatial.shape[0], frames, step, spatial.shape[3]), lambda i: (0, 0, i, 0)),
            pl.BlockSpec((H * HD, width), lambda i: (0, 0)),
        ],
        out_specs=pl.BlockSpec((frames * step, width), lambda i: (i, 0)),
        out_shape=jax.ShapeDtypeStruct((frames * patches, width), BF),
        compiler_params=pltpu.CompilerParams(vmem_limit_bytes=VMEM_LIMIT),
    )(frame_count, video, spatial, weights)


def time_kernel(count_ref, x_ref, w_ref, out_ref):
    sources, groups, rows, width = x_ref.shape
    total = sources * rows
    normed = jnp.concatenate(
        [norm_rows(x_ref[:, g].reshape(total, width).astype(F32)) for g in range(groups)], axis=0
    )
    qkv = jnp.dot(normed, w_ref[...], preferred_element_type=F32).astype(BF)
    low = lax.broadcasted_iota(jnp.int32, (total, 2 * HD), 1) < HD
    row = lax.broadcasted_iota(jnp.int32, (total, total), 0)
    col = lax.broadcasted_iota(jnp.int32, (total, total), 1)
    mask = (row % 4 == col % 4) & (col // 4 < count_ref[0])
    zero, one = jnp.zeros((total, 2 * HD), BF), jnp.ones((total, 2 * HD), BF)
    for g in range(groups):
        own = qkv[g * total : (g + 1) * total]
        scores, values = [], []
        for pair in range(H // 2):
            query, key, value = [
                own[:, k * H * HD + pair * 2 * HD : k * H * HD + (pair + 1) * 2 * HD]
                for k in range(3)
            ]
            query = (query.astype(F32) * (0.125 * LOG2E)).astype(BF)
            values += [jnp.where(low, value, one), jnp.where(low, one, value)]
            for masked in (jnp.where(low, query, zero), jnp.where(low, zero, query)):
                scores.append(
                    lax.dot_general(
                        masked, key, (((1,), (1,)), ((), ())), preferred_element_type=F32
                    )
                )
        scores = jnp.where(mask[None], jnp.stack(scores), -1e30)
        top = jnp.max(scores, axis=2, keepdims=True)
        exps = jnp.exp2((scores - top).astype(BF))
        sums = [jnp.dot(exps[h], values[h], preferred_element_type=F32) for h in range(H)]
        for pair in range(H // 2):
            first, second = sums[2 * pair], sums[2 * pair + 1]
            norm = pltpu.roll(jnp.where(low, second, first), HD, 1)
            result = (jnp.where(low, first, second) / norm).astype(BF)
            out_ref[:, g, :, pair * 2 * HD : (pair + 1) * 2 * HD] = result.reshape(
                sources, rows, 2 * HD
            )


def time_attention(frame_count, middle, weights):
    sources, groups, rows, width = middle.shape
    step = 3
    return pl.pallas_call(
        time_kernel,
        grid=(groups // step,),
        in_specs=[
            pl.BlockSpec(memory_space=pltpu.SMEM),
            pl.BlockSpec((sources, step, rows, width), lambda i: (0, i, 0, 0)),
            pl.BlockSpec((width, 3 * H * HD), lambda i: (0, 0)),
        ],
        out_specs=pl.BlockSpec((sources, step, rows, H * HD), lambda i: (0, i, 0, 0)),
        out_shape=jax.ShapeDtypeStruct((sources, groups, rows, H * HD), BF),
        compiler_params=pltpu.CompilerParams(vmem_limit_bytes=VMEM_LIMIT),
    )(frame_count, middle, weights)


def final_kernel(count_ref, m_ref, t_ref, w_ref, out_ref):
    frames, patches, width = out_ref.shape
    branch = jnp.dot(t_ref[...], w_ref[...], preferred_element_type=F32)
    first = lax.axis_index("tm") * frames
    middles = deinterleave(m_ref[...].astype(F32), frames)
    branches = deinterleave(branch, frames)
    for f in range(frames):
        valid = (first + f < count_ref[0]).astype(F32)
        out_ref[f] = (middles[f] + valid * branches[f]).astype(BF)


def final_rows(frame_count, middle, temporal, weights, frames):
    rows, width = middle.shape
    patches = rows // frames
    step = 96
    return pl.pallas_call(
        final_kernel,
        grid=(patches // step,),
        in_specs=[
            pl.BlockSpec(memory_space=pltpu.SMEM),
            pl.BlockSpec((frames * step, width), lambda i: (i, 0)),
            pl.BlockSpec((frames * step, H * HD), lambda i: (i, 0)),
            pl.BlockSpec((H * HD, width), lambda i: (0, 0)),
        ],
        out_specs=pl.BlockSpec((frames, step, width), lambda i: (0, i, 0)),
        out_shape=jax.ShapeDtypeStruct((frames, patches, width), BF),
        compiler_params=pltpu.CompilerParams(vmem_limit_bytes=VMEM_LIMIT),
    )(frame_count, middle, temporal, weights)


def by_frame(video, frame_count, qkv_space, out_space, qkv_time, out_time):
    frames, patches, width = video.shape
    devices = lax.axis_size("tm")
    spatial = space_attention(video, qkv_space)
    middle = middle_rows(frame_count, video, spatial, out_space)
    sent = middle.reshape(devices, frames * patches // devices, width)
    sent = lax.all_to_all(sent, "tm", split_axis=0, concat_axis=0, tiled=True)
    temporal = time_attention(frame_count, sent.reshape(devices, -1, 4 * frames, width), qkv_time)
    temporal = temporal.reshape(devices, frames * patches // devices, H * HD)
    temporal = lax.all_to_all(temporal, "tm", split_axis=0, concat_axis=0, tiled=True)
    return final_rows(
        frame_count, middle, temporal.reshape(frames * patches, H * HD), out_time, frames
    )


def per_device(video, *rest):
    frames, patches, _ = video.shape
    fits = (
        frames == 4
        and lax.axis_size("space") == frames
        and lax.axis_size("tm") == 8
        and patches == 288
    )
    return (by_frame if fits else general)(video, *rest)


def solution(mesh):
    return jax.shard_map(
        per_device,
        mesh=mesh,
        in_specs=(P("tm", "space", None), P(), P(), P(), P(), P()),
        out_specs=P("tm", "space", None),
        check_vma=False,
    )
```

```python
import functools
import math

import jax
import jax.numpy as jnp
from jax import lax
from jax.experimental import pallas as pl
from jax.experimental.pallas import tpu as pltpu
from jax.sharding import PartitionSpec as P

H = 16
HD = 64
BF = jnp.bfloat16
F32 = jnp.float32
VMEM_LIMIT = 56 * 1024 * 1024
LOG2E = 1.0 / math.log(2.0)


def layer_norm(values):
    wide = values.astype(jnp.float32)
    center = wide - jnp.mean(wide, axis=-1, keepdims=True)
    spread = jnp.mean(center * center, axis=-1, keepdims=True)
    return (center * lax.rsqrt(spread + 1e-06)).astype(jnp.bfloat16)


def spatial_attend(items):
    count = items.shape[0]
    total = items.shape[1]
    local_heads = items.shape[3] // HD
    parts = items.reshape(count, total, 3, local_heads, HD)
    scores = (
        jnp.einsum(
            "fqhd,fkhd->fhqk", parts[:, :, 0], parts[:, :, 1], preferred_element_type=jnp.float32
        )
        * 0.125
    )
    weights = jax.nn.softmax(scores, axis=-1).astype(jnp.bfloat16)
    result = jnp.einsum(
        "fhqk,fkhd->fqhd", weights, parts[:, :, 2], preferred_element_type=jnp.float32
    )
    result = result.astype(jnp.bfloat16).reshape(count, total, local_heads * HD)
    return lax.all_to_all(result, "space", split_axis=1, concat_axis=2, tiled=True)


def general(video, frame_count, qkv_space, out_space, qkv_time, out_time):
    frames, patches, width = video.shape
    first = lax.axis_index("tm") * frames
    limit = frame_count[0]
    valid = (first + jnp.arange(frames) < limit).astype(jnp.float32)[:, None, None]
    norm1 = layer_norm(video)
    qkv1 = jnp.dot(
        norm1.reshape(frames * patches, width), qkv_space, preferred_element_type=jnp.float32
    )
    qkv1 = qkv1.astype(jnp.bfloat16).reshape(frames, patches, 3, H * HD)
    spatial = spatial_attend(lax.all_to_all(qkv1, "space", split_axis=3, concat_axis=1, tiled=True))
    branch = jnp.dot(
        spatial.reshape(frames * patches, H * HD), out_space, preferred_element_type=jnp.float32
    )
    middle = (video.astype(jnp.float32) + valid * branch.reshape(frames, patches, width)).astype(
        jnp.bfloat16
    )
    norm2 = layer_norm(middle)
    qkv2 = jnp.dot(
        norm2.reshape(frames * patches, width), qkv_time, preferred_element_type=jnp.float32
    )
    qkv2 = qkv2.astype(jnp.bfloat16).reshape(frames, patches, 3 * H * HD)
    gathered = lax.all_to_all(qkv2, "tm", split_axis=1, concat_axis=0, tiled=True)
    all_frames, few_patches = (gathered.shape[0], gathered.shape[1])
    parts = gathered.reshape(all_frames, few_patches, 3, H, HD)
    scores = (
        jnp.einsum(
            "fphd,gphd->phfg", parts[:, :, 0], parts[:, :, 1], preferred_element_type=jnp.float32
        )
        * 0.125
    )
    key_valid = jnp.arange(all_frames) < limit
    scores = jnp.where(key_valid[None, None, None, :], scores, -1e30)
    weights = jax.nn.softmax(scores, axis=-1).astype(jnp.bfloat16)
    temporal = jnp.einsum(
        "phfg,gphd->fphd", weights, parts[:, :, 2], preferred_element_type=jnp.float32
    )
    temporal = temporal.astype(jnp.bfloat16).reshape(all_frames, few_patches, H * HD)
    returned = lax.all_to_all(temporal, "tm", split_axis=0, concat_axis=1, tiled=True)
    branch2 = jnp.dot(
        returned.reshape(frames * patches, H * HD), out_time, preferred_element_type=jnp.float32
    )
    return (middle.astype(jnp.float32) + valid * branch2.reshape(frames, patches, width)).astype(
        jnp.bfloat16
    )


def norm_rows(wide):
    center = wide - jnp.mean(wide, axis=-1, keepdims=True)
    spread = jnp.mean(center * center, axis=-1, keepdims=True)
    return (center * lax.rsqrt(spread + 1e-06)).astype(BF)


def space_kernel(video, weights, out, x_buf, w_buf, normed, qkv, sent, sems):
    send_in, recv_in, local, send_out, recv_out, keep = sems
    n, patches, width = x_buf.shape
    chunks, _, _, cols = out.shape
    me = lax.axis_index("space")
    peers = [lax.rem(me + d, n) for d in range(n)]
    froms = [lax.rem(me + n - d, n) for d in range(n)]

    barrier = pltpu.get_barrier_semaphore()
    for d in range(1, n):
        pl.semaphore_signal(
            barrier, inc=1, device_id={"space": peers[d]}, device_id_type=pl.DeviceIdType.MESH
        )
    own = pltpu.make_async_copy(video.at[me], x_buf.at[me], local.at[0])
    own.start()
    load = pltpu.make_async_copy(weights, w_buf, local.at[1])
    load.start()
    pl.semaphore_wait(barrier, n - 1)
    parts = patches // 96
    arrivals = []
    for t in range(parts):
        rows = pl.ds(t * 96, 96)
        for d in range(1, n):
            copy = pltpu.make_async_remote_copy(
                src_ref=video.at[peers[d], rows],
                dst_ref=x_buf.at[me, rows],
                send_sem=send_in.at[t, d],
                recv_sem=recv_in.at[t, d],
                device_id={"space": peers[d]},
                device_id_type=pl.DeviceIdType.MESH,
            )
            copy.start()
            arrivals.append(copy)
    own.wait()
    load.wait()

    def project(pieces):
        for at, (source, offset) in enumerate(pieces):
            rows = x_buf[source, offset : offset + 96, :]
            normed[at * 96 : (at + 1) * 96, :] = norm_rows(rows.astype(F32))

        @pl.loop(0, 6)
        def _(i):
            part = pl.ds(pl.multiple_of(i * 512, 512), 512)
            result = jnp.dot(normed[...], w_buf[:, part], preferred_element_type=F32)
            scale = jnp.where(i < 2, 0.125 * LOG2E, 1.0).astype(F32)
            result = (result * scale).astype(BF)
            for at, (source, offset) in enumerate(pieces):
                start = pl.multiple_of(source * patches + offset, 96)
                qkv[pl.ds(start, 96), part] = result[at * 96 : (at + 1) * 96]

    project([(me, t * 96) for t in range(parts)])
    for t in range(parts):
        for d in range(1, n):
            arrivals[t * (n - 1) + d - 1].wait_recv()
        project([(froms[d], t * 96) for d in range(1, n)])

    low = lax.broadcasted_iota(jnp.int32, (patches, 2 * HD), 1) < HD
    low_all = lax.broadcasted_iota(jnp.int32, (n * patches, 2 * HD), 1) < HD

    def outgoing(c, d):
        return pltpu.make_async_remote_copy(
            src_ref=sent.at[c, d],
            dst_ref=out.at[c, me],
            send_sem=send_out.at[c, d],
            recv_sem=recv_out.at[c, d],
            device_id={"space": peers[d]},
            device_id_type=pl.DeviceIdType.MESH,
        )

    @pl.loop(0, chunks)
    def _(c):
        keys, values = [], []
        for pair in range(2):
            start = pl.multiple_of(H * HD + c * cols + pair * 128, 128)
            keys.append(qkv[:, pl.ds(start, 128)])
            start = pl.multiple_of(2 * H * HD + c * cols + pair * 128, 128)
            value = qkv[:, pl.ds(start, 128)]
            one = jnp.ones_like(value)
            values.append((jnp.where(low_all, value, one), jnp.where(low_all, one, value)))
        units = [(d, pair, head) for d in (1, 2, 3, 0) for pair in range(2) for head in range(2)]

        def scores_of(unit):
            d, pair, head = unit
            rows = pl.ds(pl.multiple_of(peers[d] * patches, patches), patches)
            query = qkv[rows, pl.ds(pl.multiple_of(c * cols + pair * 128, 128), 128)]
            zero = jnp.zeros_like(query)
            query = jnp.where(low, query, zero) if head == 0 else jnp.where(low, zero, query)
            return lax.dot_general(
                query, keys[pair], (((1,), (1,)), ((), ())), preferred_element_type=F32
            )

        following = scores_of(units[0])
        sums = []
        for at, (d, pair, head) in enumerate(units):
            scores = following
            if at + 1 < len(units):
                following = scores_of(units[at + 1])
            top = jnp.max(scores, axis=1, keepdims=True)
            exps = jnp.exp2((scores - top).astype(BF))
            sums.append(jnp.dot(exps, values[pair][head], preferred_element_type=F32))
            if head == 1:
                result = jnp.where(low, sums[0], sums[1])
                norm = pltpu.roll(jnp.where(low, sums[1], sums[0]), HD, 1)
                sums = []
                sent[c, d, :, pair * 128 : (pair + 1) * 128] = (result / norm).astype(BF)
                if pair == 1:
                    if d > 0:
                        outgoing(c, d).start()
                    else:
                        pltpu.make_async_copy(sent.at[c, 0], out.at[c, me], keep.at[c]).start()

    for copy in arrivals:
        copy.wait_send()
    for c in range(chunks):
        pltpu.make_async_copy(sent.at[c, 0], out.at[c, me], keep.at[c]).wait()
        for d in range(1, n):
            outgoing(c, d).wait()


def space_attention(video, weights):
    n, patches, width = video.shape
    total = n * patches
    chunks = 4
    cols = H * HD // chunks

    def kernel(v, w, o, x_buf, w_buf, normed, qkv, sent, *sems):
        space_kernel(v, w, o, x_buf, w_buf, normed, qkv, sent, sems)

    return pl.pallas_call(
        kernel,
        in_specs=[pl.BlockSpec(memory_space=pl.ANY)] * 2,
        out_specs=pl.BlockSpec(memory_space=pl.ANY),
        out_shape=jax.ShapeDtypeStruct((chunks, n, patches, cols), BF),
        scratch_shapes=[
            pltpu.VMEM((n, patches, width), BF),
            pltpu.VMEM((width, 3 * H * HD), BF),
            pltpu.VMEM((patches, width), BF),
            pltpu.VMEM((total, 3 * H * HD), BF),
            pltpu.VMEM((chunks, n, patches, cols), BF),
            pltpu.SemaphoreType.DMA((patches // 96, n)),
            pltpu.SemaphoreType.DMA((patches // 96, n)),
            pltpu.SemaphoreType.DMA((2,)),
            pltpu.SemaphoreType.DMA((chunks, n)),
            pltpu.SemaphoreType.DMA((chunks, n)),
            pltpu.SemaphoreType.DMA((chunks,)),
        ],
        compiler_params=pltpu.CompilerParams(
            vmem_limit_bytes=VMEM_LIMIT, collective_id=0, has_side_effects=True
        ),
        cost_estimate=pl.CostEstimate(
            flops=2 * total * width * 3 * H * HD + 4 * total * total * H * HD,
            bytes_accessed=2 * (total * width + 3 * width * H * HD + total * H * HD),
            transcendentals=total * total * H,
        ),
    )(video, weights)


def interleave(values):
    frames, patches, width = values.shape
    parts = values.reshape(frames, patches // 8, 8, width)
    pieces = []
    for half in range(2):
        for f in range(frames):
            pieces.append(parts[f][:, half * 4 : half * 4 + 4])
    return jnp.concatenate(pieces, axis=1).reshape(frames * patches, width)


def deinterleave(values, frames):
    rows, width = values.shape
    parts = values.reshape(rows // (8 * frames), 8 * frames, width)
    out = []
    for f in range(frames):
        first = parts[:, f * 4 : f * 4 + 4]
        second = parts[:, 4 * frames + f * 4 : 4 * frames + f * 4 + 4]
        out.append(jnp.concatenate([first, second], axis=1).reshape(rows // frames, width))
    return out


STEP = 96
GROUPS = 3


def time_rows(x, weights, count):
    sources, every, width = x.shape
    rows = every // GROUPS
    total = sources * rows
    normed = jnp.concatenate(
        [
            norm_rows(x[:, g * rows : (g + 1) * rows].reshape(total, width).astype(F32))
            for g in range(GROUPS)
        ],
        axis=0,
    )
    qkv = jnp.dot(normed, weights[...], preferred_element_type=F32).astype(BF)
    low = lax.broadcasted_iota(jnp.int32, (total, 2 * HD), 1) < HD
    row = lax.broadcasted_iota(jnp.int32, (total, total), 0)
    col = lax.broadcasted_iota(jnp.int32, (total, total), 1)
    mask = (row % 4 == col % 4) & (col // 4 < count)
    zero, one = jnp.zeros((total, 2 * HD), BF), jnp.ones((total, 2 * HD), BF)
    for g in range(GROUPS):
        own = qkv[g * total : (g + 1) * total]
        scores, values = [], []
        for pair in range(H // 2):
            query, key, value = [
                own[:, k * H * HD + pair * 2 * HD : k * H * HD + (pair + 1) * 2 * HD]
                for k in range(3)
            ]
            query = (query.astype(F32) * (0.125 * LOG2E)).astype(BF)
            values += [jnp.where(low, value, one), jnp.where(low, one, value)]
            for masked in (jnp.where(low, query, zero), jnp.where(low, zero, query)):
                scores.append(
                    lax.dot_general(
                        masked, key, (((1,), (1,)), ((), ())), preferred_element_type=F32
                    )
                )
        scores = jnp.where(mask[None], jnp.stack(scores), -1e30)
        top = jnp.max(scores, axis=2, keepdims=True)
        exps = jnp.exp2((scores - top).astype(BF))
        sums = [jnp.dot(exps[h], values[h], preferred_element_type=F32) for h in range(H)]
        for pair in range(H // 2):
            first, second = sums[2 * pair], sums[2 * pair + 1]
            norm = pltpu.roll(jnp.where(low, second, first), HD, 1)
            result = (jnp.where(low, first, second) / norm).astype(BF)
            yield g, pair, result.reshape(sources, rows, 2 * HD)


def time_kernel(
    count_ref, video, spatial, w_space, w_qkv, w_time, out, ws, wq, wt, middle, x_in, t_out, t_in, sems
):
    loads, send_a, recv_a, send_b, recv_b = sems
    frames, patches, width = video.shape
    chunks, n, share, _ = x_in.shape
    pieces, cols = spatial.shape[0], spatial.shape[3]
    me = lax.axis_index("tm")
    peers = [lax.rem(me + d, n) for d in range(n)]
    froms = [lax.rem(me + n - d, n) for d in range(n)]
    count = count_ref[0]
    valid = [(me * frames + f < count).astype(F32) for f in range(frames)]

    barrier = pltpu.get_barrier_semaphore()
    for d in range(1, n):
        pl.semaphore_signal(
            barrier, inc=1, device_id={"tm": peers[d]}, device_id_type=pl.DeviceIdType.MESH
        )
    copies = [
        pltpu.make_async_copy(src, dst, loads.at[i])
        for i, (src, dst) in enumerate(((w_space, ws), (w_qkv, wq), (w_time, wt)))
    ]
    for copy in copies:
        copy.start()

    def forth(k, d):
        return pltpu.make_async_remote_copy(
            src_ref=middle.at[k, peers[d]],
            dst_ref=x_in.at[k, me],
            send_sem=send_a.at[k, d],
            recv_sem=recv_a.at[k, d],
            device_id={"tm": peers[d]},
            device_id_type=pl.DeviceIdType.MESH,
        )

    def back(k, d):
        return pltpu.make_async_remote_copy(
            src_ref=t_out.at[k, peers[d]],
            dst_ref=t_in.at[k, me],
            send_sem=send_b.at[k, d],
            recv_sem=recv_b.at[k, d],
            device_id={"tm": peers[d]},
            device_id_type=pl.DeviceIdType.MESH,
        )

    pl.semaphore_wait(barrier, n - 1)
    copies[0].wait()

    @pl.loop(0, chunks)
    def _(k):
        part = pl.ds(pl.multiple_of(k * STEP, STEP), STEP)
        branch = sum(
            jnp.dot(
                spatial[c, :, part, :].reshape(frames * STEP, cols),
                ws[c * cols : (c + 1) * cols, :],
                preferred_element_type=F32,
            )
            for c in range(pieces)
        ).reshape(frames, STEP, width)
        wide = [video[f, part, :].astype(F32) + valid[f] * branch[f] for f in range(frames)]
        middle[k] = interleave(jnp.stack(wide)).astype(BF).reshape(n, share, width)
        for d in range(1, n):
            forth(k, d).start()
        x_in[k, me] = middle[k, me]

    copies[1].wait()

    @pl.loop(0, chunks)
    def _(k):
        for d in range(1, n):
            forth(k, d).wait_recv()
        rows = share // GROUPS
        for g, pair, result in time_rows(x_in[k], wq, count):
            t_out[k, :, g * rows : (g + 1) * rows, pair * 2 * HD : (pair + 1) * 2 * HD] = result
        for d in range(1, n):
            back(k, d).start()
        t_in[k, me] = t_out[k, me]

    copies[2].wait()

    @pl.loop(0, chunks)
    def _(k):
        for d in range(1, n):
            back(k, d).wait_recv()
        branch = jnp.dot(
            t_in[k].reshape(n * share, H * HD), wt[...], preferred_element_type=F32
        )
        middles = deinterleave(middle[k].reshape(n * share, width).astype(F32), frames)
        branches = deinterleave(branch, frames)
        part = pl.ds(pl.multiple_of(k * STEP, STEP), STEP)
        for f in range(frames):
            out[f, part, :] = (middles[f] + valid[f] * branches[f]).astype(BF)

    @pl.loop(0, chunks)
    def _(k):
        for d in range(1, n):
            forth(k, d).wait_send()
            back(k, d).wait_send()


def time_part(frame_count, video, spatial, w_space, w_qkv, w_time):
    frames, patches, width = video.shape
    n = lax.axis_size("tm")
    chunks = patches // STEP
    share = frames * STEP // n

    def kernel(*refs):
        time_kernel(*refs[:14], refs[14:])

    vmem = pl.BlockSpec(memory_space=pltpu.VMEM)
    hbm = pl.BlockSpec(memory_space=pl.ANY)
    tokens = frames * patches
    return pl.pallas_call(
        kernel,
        in_specs=[pl.BlockSpec(memory_space=pltpu.SMEM), vmem, vmem, hbm, hbm, hbm],
        out_specs=vmem,
        out_shape=jax.ShapeDtypeStruct(video.shape, BF),
        scratch_shapes=[
            pltpu.VMEM(w_space.shape, BF),
            pltpu.VMEM(w_qkv.shape, BF),
            pltpu.VMEM(w_time.shape, BF),
            pltpu.VMEM((chunks, n, share, width), BF),
            pltpu.VMEM((chunks, n, share, width), BF),
            pltpu.VMEM((chunks, n, share, H * HD), BF),
            pltpu.VMEM((chunks, n, share, H * HD), BF),
            pltpu.SemaphoreType.DMA((3,)),
            pltpu.SemaphoreType.DMA((chunks, n)),
            pltpu.SemaphoreType.DMA((chunks, n)),
            pltpu.SemaphoreType.DMA((chunks, n)),
            pltpu.SemaphoreType.DMA((chunks, n)),
        ],
        compiler_params=pltpu.CompilerParams(
            vmem_limit_bytes=VMEM_LIMIT, collective_id=1, has_side_effects=True
        ),
        cost_estimate=pl.CostEstimate(
            flops=2 * tokens * width * 5 * H * HD + 4 * tokens * 128 * H * HD,
            bytes_accessed=2 * (2 * tokens * width + tokens * H * HD + 5 * width * H * HD),
            transcendentals=tokens * 128 * H,
        ),
    )(frame_count, video, spatial, w_space, w_qkv, w_time)


def by_frame(video, frame_count, qkv_space, out_space, qkv_time, out_time):
    spatial = space_attention(video, qkv_space)
    return time_part(frame_count, video, spatial, out_space, qkv_time, out_time)


def per_device(video, *rest):
    frames, patches, _ = video.shape
    fits = (
        frames == 4
        and lax.axis_size("space") == frames
        and lax.axis_size("tm") == 8
        and patches == 288
    )
    return (by_frame if fits else general)(video, *rest)


def solution(mesh):
    return jax.shard_map(
        per_device,
        mesh=mesh,
        in_specs=(P("tm", "space", None), P(), P(), P(), P(), P()),
        out_specs=P("tm", "space", None),
        check_vma=False,
    )
```

```python
import math

import jax
import jax.numpy as jnp
from jax import lax
from jax.experimental import pallas as pl
from jax.experimental.pallas import tpu as pltpu
from jax.sharding import PartitionSpec as P

H = 16
HD = 64
BF = jnp.bfloat16
F32 = jnp.float32
VMEM_LIMIT = 62 * 1024 * 1024
LOG2E = 1.0 / math.log(2.0)


def layer_norm(values):
    wide = values.astype(jnp.float32)
    center = wide - jnp.mean(wide, axis=-1, keepdims=True)
    spread = jnp.mean(center * center, axis=-1, keepdims=True)
    return (center * lax.rsqrt(spread + 1e-06)).astype(jnp.bfloat16)


def spatial_attend(items):
    count = items.shape[0]
    total = items.shape[1]
    local_heads = items.shape[3] // HD
    parts = items.reshape(count, total, 3, local_heads, HD)
    scores = (
        jnp.einsum(
            "fqhd,fkhd->fhqk", parts[:, :, 0], parts[:, :, 1], preferred_element_type=jnp.float32
        )
        * 0.125
    )
    weights = jax.nn.softmax(scores, axis=-1).astype(jnp.bfloat16)
    result = jnp.einsum(
        "fhqk,fkhd->fqhd", weights, parts[:, :, 2], preferred_element_type=jnp.float32
    )
    result = result.astype(jnp.bfloat16).reshape(count, total, local_heads * HD)
    return lax.all_to_all(result, "space", split_axis=1, concat_axis=2, tiled=True)


def general(video, frame_count, qkv_space, out_space, qkv_time, out_time):
    frames, patches, width = video.shape
    first = lax.axis_index("tm") * frames
    limit = frame_count[0]
    valid = (first + jnp.arange(frames) < limit).astype(jnp.float32)[:, None, None]
    norm1 = layer_norm(video)
    qkv1 = jnp.dot(
        norm1.reshape(frames * patches, width), qkv_space, preferred_element_type=jnp.float32
    )
    qkv1 = qkv1.astype(jnp.bfloat16).reshape(frames, patches, 3, H * HD)
    spatial = spatial_attend(lax.all_to_all(qkv1, "space", split_axis=3, concat_axis=1, tiled=True))
    branch = jnp.dot(
        spatial.reshape(frames * patches, H * HD), out_space, preferred_element_type=jnp.float32
    )
    middle = (video.astype(jnp.float32) + valid * branch.reshape(frames, patches, width)).astype(
        jnp.bfloat16
    )
    norm2 = layer_norm(middle)
    qkv2 = jnp.dot(
        norm2.reshape(frames * patches, width), qkv_time, preferred_element_type=jnp.float32
    )
    qkv2 = qkv2.astype(jnp.bfloat16).reshape(frames, patches, 3 * H * HD)
    gathered = lax.all_to_all(qkv2, "tm", split_axis=1, concat_axis=0, tiled=True)
    all_frames, few_patches = (gathered.shape[0], gathered.shape[1])
    parts = gathered.reshape(all_frames, few_patches, 3, H, HD)
    scores = (
        jnp.einsum(
            "fphd,gphd->phfg", parts[:, :, 0], parts[:, :, 1], preferred_element_type=jnp.float32
        )
        * 0.125
    )
    key_valid = jnp.arange(all_frames) < limit
    scores = jnp.where(key_valid[None, None, None, :], scores, -1e30)
    weights = jax.nn.softmax(scores, axis=-1).astype(jnp.bfloat16)
    temporal = jnp.einsum(
        "phfg,gphd->fphd", weights, parts[:, :, 2], preferred_element_type=jnp.float32
    )
    temporal = temporal.astype(jnp.bfloat16).reshape(all_frames, few_patches, H * HD)
    returned = lax.all_to_all(temporal, "tm", split_axis=0, concat_axis=1, tiled=True)
    branch2 = jnp.dot(
        returned.reshape(frames * patches, H * HD), out_time, preferred_element_type=jnp.float32
    )
    return (middle.astype(jnp.float32) + valid * branch2.reshape(frames, patches, width)).astype(
        jnp.bfloat16
    )


def norm_rows(wide):
    center = wide - jnp.mean(wide, axis=-1, keepdims=True)
    spread = jnp.mean(center * center, axis=-1, keepdims=True)
    return (center * lax.rsqrt(spread + 1e-06)).astype(BF)


def interleave(values):
    frames, patches, width = values.shape
    parts = values.reshape(frames, patches // 8, 8, width)
    pieces = []
    for half in range(2):
        for f in range(frames):
            pieces.append(parts[f][:, half * 4 : half * 4 + 4])
    return jnp.concatenate(pieces, axis=1).reshape(frames * patches, width)


def deinterleave(values, frames):
    rows, width = values.shape
    parts = values.reshape(rows // (8 * frames), 8 * frames, width)
    out = []
    for f in range(frames):
        first = parts[:, f * 4 : f * 4 + 4]
        second = parts[:, 4 * frames + f * 4 : 4 * frames + f * 4 + 4]
        out.append(jnp.concatenate([first, second], axis=1).reshape(rows // frames, width))
    return out


STEP = 96
GROUPS = 3


def time_rows(x, weights, count):
    sources, every, width = x.shape
    rows = every // GROUPS
    total = sources * rows
    normed = jnp.concatenate(
        [
            norm_rows(x[:, g * rows : (g + 1) * rows].reshape(total, width).astype(F32))
            for g in range(GROUPS)
        ],
        axis=0,
    )
    qkv = jnp.dot(normed, weights[...], preferred_element_type=F32).astype(BF)
    low = lax.broadcasted_iota(jnp.int32, (total, 2 * HD), 1) < HD
    row = lax.broadcasted_iota(jnp.int32, (total, total), 0)
    col = lax.broadcasted_iota(jnp.int32, (total, total), 1)
    mask = (row % 4 == col % 4) & (col // 4 < count)
    zero, one = jnp.zeros((total, 2 * HD), BF), jnp.ones((total, 2 * HD), BF)
    for g in range(GROUPS):
        own = qkv[g * total : (g + 1) * total]
        scores, values = [], []
        for pair in range(H // 2):
            query, key, value = [
                own[:, k * H * HD + pair * 2 * HD : k * H * HD + (pair + 1) * 2 * HD]
                for k in range(3)
            ]
            query = (query.astype(F32) * (0.125 * LOG2E)).astype(BF)
            values += [jnp.where(low, value, one), jnp.where(low, one, value)]
            for masked in (jnp.where(low, query, zero), jnp.where(low, zero, query)):
                scores.append(
                    lax.dot_general(
                        masked, key, (((1,), (1,)), ((), ())), preferred_element_type=F32
                    )
                )
        scores = jnp.where(mask[None], jnp.stack(scores), -1e30)
        top = jnp.max(scores, axis=2, keepdims=True)
        exps = jnp.exp2((scores - top).astype(BF))
        sums = [jnp.dot(exps[h], values[h], preferred_element_type=F32) for h in range(H)]
        for pair in range(H // 2):
            first, second = sums[2 * pair], sums[2 * pair + 1]
            norm = pltpu.roll(jnp.where(low, second, first), HD, 1)
            result = (jnp.where(low, first, second) / norm).astype(BF)
            yield g, pair, result.reshape(sources, rows, 2 * HD)


def block_kernel(
    count_ref, video_hbm, video, w_space, w_os, w_time, w_ot, out,
    x_buf, w_buf, normed, qkv, sent, spatial, ws, wt, middle, x_in, t_out, t_in,
    loads, sem_v, sem_s, sem_a, sem_b,
):
    n, patches, width = x_buf.shape
    chunks, pieces, _, _, cols = spatial.shape
    devices, share = x_in.shape[1], x_in.shape[2]
    z_me, t_me = lax.axis_index("space"), lax.axis_index("tm")
    z_to = [lax.rem(z_me + d, n) for d in range(n)]
    z_from = [lax.rem(z_me + n - d, n) for d in range(n)]
    t_to = [lax.rem(t_me + d, devices) for d in range(devices)]
    count = count_ref[0]
    valid = [(t_me * n + f < count).astype(F32) for f in range(n)]

    barrier = pltpu.get_barrier_semaphore()
    for axis, peers in (("space", z_to), ("tm", t_to)):
        for peer in peers[1:]:
            pl.semaphore_signal(
                barrier, inc=1, device_id={axis: peer}, device_id_type=pl.DeviceIdType.MESH
            )
    own = pltpu.make_async_copy(video_hbm.at[z_me], x_buf.at[z_me], loads.at[0])
    own.start()
    load = pltpu.make_async_copy(w_space, w_buf, loads.at[1])
    load.start()
    load_s = pltpu.make_async_copy(w_os, ws, loads.at[2])
    load_t = pltpu.make_async_copy(w_ot, wt, loads.at[3])
    pl.semaphore_wait(barrier, n + devices - 2)

    def remote(src, dst, sems, i, d, axis, peer):
        return pltpu.make_async_remote_copy(
            src_ref=src,
            dst_ref=dst,
            send_sem=sems.at[0, i, d],
            recv_sem=sems.at[1, i, d],
            device_id={axis: peer},
            device_id_type=pl.DeviceIdType.MESH,
        )

    def rows_in(t, d):
        rows = pl.ds(t * STEP, STEP)
        return remote(
            video_hbm.at[z_to[d], rows], x_buf.at[z_me, rows], sem_v, t, d, "space", z_to[d]
        )

    def result_back(k, c, d):
        return remote(
            sent.at[k, c, d], spatial.at[k, c, z_me], sem_s, k * pieces + c, d, "space", z_to[d]
        )

    def forth(k, d):
        return remote(middle.at[k, t_to[d]], x_in.at[k, t_me], sem_a, k, d, "tm", t_to[d])

    def back(k, d):
        return remote(t_out.at[k, t_to[d]], t_in.at[k, t_me], sem_b, k, d, "tm", t_to[d])

    for t in range(chunks):
        for d in range(1, n):
            rows_in(t, d).start()
    load_s.start()
    load_t.start()
    own.wait()
    load.wait()

    def project(blocks):
        for at, (source, offset) in enumerate(blocks):
            rows = x_buf[source, offset : offset + STEP, :]
            normed[at * STEP : (at + 1) * STEP, :] = norm_rows(rows.astype(F32))

        @pl.loop(0, 6)
        def _(i):
            part = pl.ds(pl.multiple_of(i * 512, 512), 512)
            result = jnp.dot(normed[...], w_buf[:, part], preferred_element_type=F32)
            scale = jnp.where(i < 2, 0.125 * LOG2E, 1.0).astype(F32)
            result = (result * scale).astype(BF)
            for at, (source, offset) in enumerate(blocks):
                start = pl.multiple_of(source * patches + offset, STEP)
                qkv[pl.ds(start, STEP), part] = result[at * STEP : (at + 1) * STEP]

    project([(z_me, t * STEP) for t in range(chunks)])
    for t in range(chunks):
        for d in range(1, n):
            rows_in(t, d).wait_recv()
        project([(z_from[d], t * STEP) for d in range(1, n)])
    load_q = pltpu.make_async_copy(w_time, w_buf, loads.at[4])
    load_q.start()

    low = lax.broadcasted_iota(jnp.int32, (n * STEP, 2 * HD), 1) < HD
    low_all = lax.broadcasted_iota(jnp.int32, (n * patches, 2 * HD), 1) < HD

    def attend(k):
        @pl.loop(0, pieces)
        def _(c):
            keys, values, queries = [], [], []
            for pair in range(2):
                start = pl.multiple_of(c * cols + pair * 128, 128)
                query = jnp.concatenate(
                    [
                        qkv[
                            pl.ds(pl.multiple_of(z_to[d] * patches + k * STEP, STEP), STEP),
                            pl.ds(start, 128),
                        ]
                        for d in range(n)
                    ],
                    axis=0,
                )
                zero = jnp.zeros_like(query)
                queries.append((jnp.where(low, query, zero), jnp.where(low, zero, query)))
                keys.append(qkv[:, pl.ds(pl.multiple_of(start + H * HD, 128), 128)])
                value = qkv[:, pl.ds(pl.multiple_of(start + 2 * H * HD, 128), 128)]
                one = jnp.ones_like(value)
                values.append((jnp.where(low_all, value, one), jnp.where(low_all, one, value)))

            def scores_of(pair, head):
                return lax.dot_general(
                    queries[pair][head],
                    keys[pair],
                    (((1,), (1,)), ((), ())),
                    preferred_element_type=F32,
                )

            units = [(pair, head) for pair in range(2) for head in range(2)]
            following = scores_of(*units[0])
            sums = []
            for at, (pair, head) in enumerate(units):
                scores = following
                if at + 1 < len(units):
                    following = scores_of(*units[at + 1])
                top = jnp.max(scores, axis=1, keepdims=True)
                exps = jnp.exp2((scores - top).astype(BF))
                sums.append(jnp.dot(exps, values[pair][head], preferred_element_type=F32))
                if head == 1:
                    result = jnp.where(low, sums[0], sums[1])
                    norm = pltpu.roll(jnp.where(low, sums[1], sums[0]), HD, 1)
                    sums = []
                    result = (result / norm).astype(BF)
                    place = slice(pair * 128, (pair + 1) * 128)
                    spatial[k, c, z_me, :, place] = result[:STEP]
                    for d in range(1, n):
                        sent[k, c, d, :, place] = result[d * STEP : (d + 1) * STEP]
            for d in range(1, n):
                result_back(k, c, d).start()

    def join(k):
        @pl.loop(0, pieces)
        def _(c):
            for d in range(1, n):
                result_back(k, c, d).wait_recv()

        part = slice(k * STEP, (k + 1) * STEP)
        branch = sum(
            jnp.dot(
                spatial[k, c].reshape(n * STEP, cols),
                ws[c * cols : (c + 1) * cols, :],
                preferred_element_type=F32,
            )
            for c in range(pieces)
        ).reshape(n, STEP, width)
        wide = [video[f, part, :].astype(F32) + valid[f] * branch[f] for f in range(n)]
        middle[k] = interleave(jnp.stack(wide)).astype(BF).reshape(devices, share, width)
        for d in range(1, devices):
            forth(k, d).start()
        x_in[k, t_me] = middle[k, t_me]

    def over_time(k):
        for d in range(1, devices):
            forth(k, d).wait_recv()
        rows = share // GROUPS
        for g, pair, result in time_rows(x_in[k], w_buf, count):
            t_out[k, :, g * rows : (g + 1) * rows, pair * 2 * HD : (pair + 1) * 2 * HD] = result
        for d in range(1, devices):
            back(k, d).start()
        t_in[k, t_me] = t_out[k, t_me]

    def finish(k):
        for d in range(1, devices):
            back(k, d).wait_recv()
        branch = jnp.dot(
            t_in[k].reshape(devices * share, H * HD), wt[...], preferred_element_type=F32
        )
        middles = deinterleave(middle[k].reshape(devices * share, width).astype(F32), n)
        branches = deinterleave(branch, n)
        for f in range(n):
            out[f, k * STEP : (k + 1) * STEP, :] = (middles[f] + valid[f] * branches[f]).astype(BF)

    attend(0)
    attend(1)
    load_s.wait()
    join(0)
    attend(2)
    join(1)
    load_q.wait()
    over_time(0)
    join(2)
    over_time(1)
    over_time(2)
    load_t.wait()
    finish(0)
    finish(1)
    finish(2)

    for t in range(chunks):
        for d in range(1, n):
            rows_in(t, d).wait_send()
            for c in range(pieces):
                result_back(t, c, d).wait_send()
        for d in range(1, devices):
            forth(t, d).wait_send()
            back(t, d).wait_send()


def by_frame(video, frame_count, qkv_space, out_space, qkv_time, out_time):
    n, patches, width = video.shape
    devices = lax.axis_size("tm")
    chunks, pieces = patches // STEP, 4
    share = n * STEP // devices
    tokens = n * patches
    cols = H * HD // pieces
    vmem = pl.BlockSpec(memory_space=pltpu.VMEM)
    hbm = pl.BlockSpec(memory_space=pl.ANY)
    return pl.pallas_call(
        block_kernel,
        in_specs=[pl.BlockSpec(memory_space=pltpu.SMEM), hbm, vmem, hbm, hbm, hbm, hbm],
        out_specs=vmem,
        out_shape=jax.ShapeDtypeStruct(video.shape, BF),
        scratch_shapes=[
            pltpu.VMEM((n, patches, width), BF),
            pltpu.VMEM(qkv_space.shape, BF),
            pltpu.VMEM((patches, width), BF),
            pltpu.VMEM((tokens, 3 * H * HD), BF),
            pltpu.VMEM((chunks, pieces, n, STEP, cols), BF),
            pltpu.VMEM((chunks, pieces, n, STEP, cols), BF),
            pltpu.VMEM(out_space.shape, BF),
            pltpu.VMEM(out_time.shape, BF),
            pltpu.VMEM((chunks, devices, share, width), BF),
            pltpu.VMEM((chunks, devices, share, width), BF),
            pltpu.VMEM((chunks, devices, share, H * HD), BF),
            pltpu.VMEM((chunks, devices, share, H * HD), BF),
            pltpu.SemaphoreType.DMA((5,)),
            pltpu.SemaphoreType.DMA((2, chunks, n)),
            pltpu.SemaphoreType.DMA((2, chunks * pieces, n)),
            pltpu.SemaphoreType.DMA((2, chunks, devices)),
            pltpu.SemaphoreType.DMA((2, chunks, devices)),
        ],
        compiler_params=pltpu.CompilerParams(
            vmem_limit_bytes=VMEM_LIMIT, collective_id=0, has_side_effects=True
        ),
        cost_estimate=pl.CostEstimate(
            flops=16 * tokens * width * H * HD + 4 * tokens * (tokens + 128) * H * HD,
            bytes_accessed=2 * (3 * tokens * width + 8 * width * H * HD),
            transcendentals=tokens * (tokens + 128) * H,
        ),
    )(frame_count, video, video, qkv_space, out_space, qkv_time, out_time)


def per_device(video, *rest):
    frames, patches, _ = video.shape
    fits = (
        frames == 4
        and lax.axis_size("space") == frames
        and lax.axis_size("tm") == 8
        and patches == 288
    )
    return (by_frame if fits else general)(video, *rest)


def solution(mesh):
    return jax.shard_map(
        per_device,
        mesh=mesh,
        in_specs=(P("tm", "space", None), P(), P(), P(), P(), P()),
        out_specs=P("tm", "space", None),
        check_vma=False,
    )
```
